32 devices in a mesh: dp: 1, dap: 32 (over z, y, x, core).
Axes of the slice: x: 2, y: 2, z: 4, core: 2. Of those that a mesh axis runs over, the one named last changes fastest.
Arguments:
- alignment: bfloat16 [128, 256, 256], P(('dp', 'dap')), may hold values from -6 to 6
- pair_rep: bfloat16 [256, 256, 128], P(('dp', 'dap')), may hold values from -6 to 6
- align_mask: int32 [128, 256], P(('dp', 'dap')), may hold values 0 or 1
- residue_mask: int32 [256], P('dp'), may hold values 0 or 1
- row_gain: float32 [256], replicated, may hold values from 0.1 to 1.9
- pair_gain: float32 [128], replicated, may hold values from 0.1 to 1.9
- row_bias: bfloat16 [128, 8], replicated, may hold values from -0.5 to 0.5
- row_scoring: bfloat16 [256, 512], replicated, may hold values from -4 to 4
- row_values: bfloat16 [256, 512], replicated, may hold values from -0.375 to 0.375
- row_output: bfloat16 [256, 256], replicated, may hold values from -0.375 to 0.375
- column_gain: float32 [256], replicated, may hold values from 0.1 to 1.9
- column_scoring: bfloat16 [256, 512], replicated, may hold values from -4 to 4
- column_values: bfloat16 [256, 512], replicated, may hold values from -0.375 to 0.375
- column_output: bfloat16 [256, 256], replicated, may hold values from -0.375 to 0.375
- outer_gain: float32 [256], replicated, may hold values from 0.1 to 1.9
- outer_inputs: bfloat16 [256, 64], replicated, may hold values from -0.375 to 0.375
- outer_output: bfloat16 [1024, 128], replicated, may hold values from -1 to 1
Outputs:
- new_alignment: bfloat16 [128, 256, 256], P(('dp', 'dap'))
- new_pair: bfloat16 [256, 256, 128], P(('dp', 'dap'))
The draws below stay inside these ranges and needn't reach their ends.
All inputs are finite; a program needn't handle non-finite values. No bound on the sum of `align_mask` on one device may be relied on, other than what follows from the above.
Results may differ from the reference program's by a relative error of at most 0.012.
The reference program's roundings to bfloat16 on the way count: a program that leaves them out, or rounds other values in their place, can miss the bound.
Values may be sent and summed in bfloat16 or wider, within the bound.
A program may use at most 64 MiB of HBM per device.

```python
import math
import jax
import jax.numpy as jnp
from jax import lax

C_M = 256
C_Z = 128
HEADS = 8
HEAD = 32
C_OPM = 32
N_SEQ = 128
N_RES = 256


def query_key(key):
    base = jax.random.normal(jax.random.fold_in(key, 11), (C_M, C_M), jnp.float32)
    other = jax.random.normal(jax.random.fold_in(key, 14), (C_M, C_M), jnp.float32)
    query_part = base * C_M ** (-0.5)
    key_part = other * C_M ** (-0.5)
    joined = jnp.clip(jnp.concatenate([query_part, key_part], axis=1), -4.0, 4.0)
    return joined.astype(jnp.bfloat16)


def draw_row_scoring(key, part):
    return query_key(jax.random.fold_in(key, 1))


def draw_column_scoring(key, part):
    return query_key(jax.random.fold_in(key, 2))


def with_ends(array, own_key, low, largest):
    longest = array.shape.index(max(array.shape))
    spots = []
    for shift in (0, 1):
        where = [jax.random.randint(jax.random.fold_in(own_key, axis), (), 0, length) for axis, length in enumerate(array.shape)]
        where[longest] = (where[longest] + shift) % array.shape[longest]
        spots.append(tuple(where))
    return array.at[spots[0]].set(low).at[spots[1]].set(largest)


def steps_of(rng, dims, cuts, smallest, largest):
    def one(dim, blocks):
        steps = jax.random.uniform(jax.random.fold_in(jax.random.fold_in(rng, 6), dim), (blocks,), jnp.float32, smallest / len(cuts), largest / len(cuts))
        return jnp.repeat(jnp.exp(steps), dims[dim] // blocks).reshape((-1,) + (1,) * (len(dims) - dim - 1))

    level = one(*cuts[0])
    for cut in cuts[1:]:
        level = level * one(*cut)
    return level


def scatter_about(stream_key, extent, deviation, bound, cuts=(), kind=jnp.bfloat16):
    result = jax.random.normal(stream_key, extent, jnp.float32) * deviation
    if len(cuts) > 0:
        result = steps_of(stream_key, extent, cuts, -0.22, 0.18) * result
    return jnp.clip(result, min=-bound, max=bound).astype(kind)


def setup_inputs(seed: int = 0, part: int = 0) -> dict:
    arg_keys = jax.random.split(jax.random.key(seed), 18)
    part_keys = jax.random.split(jax.random.fold_in(arg_keys[17], part), 18)
    return {
        "alignment": scatter_about(part_keys[0], (N_SEQ, N_RES, C_M), 1.0, 6.0, ((0, 32),)),
        "pair_rep": scatter_about(part_keys[1], (N_RES, N_RES, C_Z), 1.0, 6.0, ((0, 32),)),
        "align_mask": with_ends((jax.random.randint(part_keys[2], (N_SEQ, N_RES), 0, 8) < 7).astype(jnp.int32), jax.random.fold_in(part_keys[2], 1), 0, 1),
        "residue_mask": with_ends((jax.random.randint(part_keys[3], (N_RES,), 0, 16) < 15).astype(jnp.int32), jax.random.fold_in(part_keys[3], 1), 0, 1),
        "row_gain": jnp.clip(1.0 + 0.18 * jax.random.normal(arg_keys[4], (C_M,), jnp.float32), 0.1, 1.9),
        "pair_gain": jnp.clip(1.0 + 0.18 * jax.random.normal(arg_keys[5], (C_Z,), jnp.float32), 0.1, 1.9),
        "row_bias": scatter_about(arg_keys[6], (C_Z, HEADS), C_Z ** -0.5, 0.5),
        "row_scoring": draw_row_scoring(jax.random.fold_in(arg_keys[17], 71), part),
        "row_values": scatter_about(arg_keys[8], (C_M, 2 * C_M), C_M ** -0.5, 0.375),
        "row_output": scatter_about(arg_keys[9], (C_M, C_M), C_M ** -0.5, 0.375),
        "column_gain": jnp.clip(1.0 + 0.18 * jax.random.normal(arg_keys[10], (C_M,), jnp.float32), 0.1, 1.9),
        "column_scoring": draw_column_scoring(jax.random.fold_in(arg_keys[17], 71), part),
        "column_values": scatter_about(arg_keys[12], (C_M, 2 * C_M), C_M ** -0.5, 0.375),
        "column_output": scatter_about(arg_keys[13], (C_M, C_M), C_M ** -0.5, 0.375),
        "outer_gain": jnp.clip(1.0 + 0.18 * jax.random.normal(arg_keys[14], (C_M,), jnp.float32), 0.1, 1.9),
        "outer_inputs": scatter_about(arg_keys[15], (C_M, 2 * C_OPM), C_M ** -0.5, 0.375),
        "outer_output": scatter_about(arg_keys[16], (C_OPM * C_OPM, C_Z), C_OPM ** -0.5, 1.0),
    }


def layer_norm(values_in, gain):
    wide = values_in.astype(jnp.float32)
    average = lax.optimization_barrier(jnp.mean(wide, axis=-1, keepdims=True))
    centred = wide - average
    spread = lax.optimization_barrier(jnp.mean(centred * centred, axis=-1, keepdims=True))
    return (centred * lax.rsqrt(spread + 1e-05) * gain).astype(jnp.bfloat16)

def linear(inputs, weight):
    return jnp.einsum('...c,cd->...d', inputs.astype(jnp.float32), weight.astype(jnp.float32))

def attend_one(queries, keys_all, values_all, gates, keep_mask, bias_term):
    length_q = queries.shape[0]
    length_k = keys_all.shape[0]
    heads_q = queries.astype(jnp.float32).reshape(length_q, HEADS, HEAD)
    heads_k = keys_all.astype(jnp.float32).reshape(length_k, HEADS, HEAD)
    heads_v = values_all.astype(jnp.float32).reshape(length_k, HEADS, HEAD)
    scores = jnp.einsum('ihd,jhd->hij', heads_q, heads_k) / math.sqrt(HEAD) + bias_term
    scores = jnp.where(keep_mask[None, None, :] > 0, scores, -1000000000.0)
    weights = jax.nn.softmax(scores, axis=-1).astype(jnp.bfloat16)
    mixed = jnp.einsum('hij,jhd->ihd', weights.astype(jnp.float32), heads_v).reshape(length_q, HEADS * HEAD)
    return (mixed * jax.nn.sigmoid(gates.astype(jnp.float32))).astype(jnp.bfloat16)

def attention_layer(stream, gain, scoring, valuing, output, keep_mask, bias_term):
    normed = layer_norm(stream, gain)
    joint = linear(normed, scoring).astype(jnp.bfloat16)
    gated = linear(normed, valuing).astype(jnp.bfloat16)
    queries, keys_all = (joint[..., :C_M], joint[..., C_M:])
    values_all, gates = (gated[..., :C_M], gated[..., C_M:])

    def single(item):
        return attend_one(item[0], item[1], item[2], item[3], item[4], bias_term)
    mixed = lax.map(single, (queries, keys_all, values_all, gates, keep_mask))
    return (stream.astype(jnp.float32) + linear(mixed, output)).astype(jnp.bfloat16)

def reference(alignment, pair_rep, align_mask, residue_mask, row_gain, pair_gain, row_bias, row_scoring, row_values, row_output, column_gain, column_scoring, column_values, column_output, outer_gain, outer_inputs, outer_output):
    mask_float = align_mask.astype(jnp.float32)
    mask_narrow = align_mask.astype(jnp.bfloat16)
    residue_float = residue_mask.astype(jnp.float32)
    pair_bias = linear(layer_norm(pair_rep, pair_gain), row_bias).astype(jnp.bfloat16)
    bias_heads = jnp.transpose(pair_bias, (2, 0, 1)).astype(jnp.float32)
    keep_rows = mask_float * residue_float[None, :]
    first_update = attention_layer(alignment, row_gain, row_scoring, row_values, row_output, keep_rows, bias_heads)
    turned = jnp.swapaxes(first_update, 0, 1)
    second = attention_layer(turned, column_gain, column_scoring, column_values, column_output, jnp.swapaxes(mask_float, 0, 1), jnp.float32(0.0))
    new_alignment = jnp.swapaxes(second, 0, 1)
    outer_normed = layer_norm(new_alignment, outer_gain)
    sides = (linear(outer_normed, outer_inputs) * mask_float[..., None]).astype(jnp.bfloat16)
    left_side = sides[..., :C_OPM]
    right_side = sides[..., C_OPM:].astype(jnp.float32)
    pair_count = jnp.dot(jnp.swapaxes(mask_narrow, 0, 1), mask_narrow, preferred_element_type=jnp.float32)

    def one_row(item):
        left_row, count_row, pair_row, factor = item
        products = jnp.einsum('sc,sje->jce', left_row.astype(jnp.float32), right_side).astype(jnp.bfloat16)
        projected = jnp.dot(products.reshape(N_RES, C_OPM * C_OPM), outer_output, preferred_element_type=jnp.float32)
        scaled = projected / (0.001 + count_row)[:, None] * factor * residue_float[:, None]
        return (pair_row.astype(jnp.float32) + scaled).astype(jnp.bfloat16)
    new_pair = lax.map(one_row, (jnp.swapaxes(left_side, 0, 1), pair_count, pair_rep, residue_float))
    return (new_alignment, new_pair)
```

```python
import functools
import math

import jax
import jax.numpy as jnp
from jax import lax
from jax.experimental import pallas as pl
from jax.experimental.pallas import tpu as pltpu
from jax.sharding import PartitionSpec as P

HEADS = 8
HEAD = 32
C_OPM = 32
LOG2E = math.log2(math.e)
SCALE = LOG2E / math.sqrt(HEAD)
MASKED = -1000000000.0 * LOG2E
NT = (((1,), (1,)), ((), ()))
MESH = pl.DeviceIdType.MESH
VMEM = pl.BlockSpec(memory_space=pltpu.VMEM)
LIMIT = 60 * 1024 * 1024
narrow, full = jnp.bfloat16, jnp.float32


def norm(wide, gain):
    average = jnp.mean(wide, axis=-1, keepdims=True)
    centred = wide - average
    spread = jnp.mean(centred * centred, axis=-1, keepdims=True)
    return (centred * lax.rsqrt(spread + 1e-05) * gain).astype(narrow)


def dot(a, b):
    return jnp.dot(a, b, preferred_element_type=full)


def dot_nt(a, b):
    return lax.dot_general(a, b, NT, preferred_element_type=full)


def flip(b, bit):
    return b + bit - 2 * bit * lax.rem(b // bit, 2)


class Place:
    def __init__(self, me):
        self.me, self.core = me, lax.rem(me, 2)
        self.far, self.near = flip(me, 16), flip(me, 8)
        self.partners = (self.f(me), self.g(me), flip(me, 1), self.far, self.near)

    def f(self, b):
        x, y = 2 - 4 * lax.rem(b // 2, 2), 4 - 8 * lax.rem(b // 4, 2)
        return b + (1 - self.core) * x + self.core * y

    def g(self, b):
        x, y = 2 - 4 * lax.rem(b // 2, 2), 4 - 8 * lax.rem(b // 4, 2)
        return b + self.core * x + (1 - self.core) * y

    def layer(self, b, d):
        if d % 2:
            b = flip(b, 16)
        return flip(b, 8) if d >= 2 else b


def greet(place):
    barrier = pltpu.get_barrier_semaphore()
    for target in place.partners:
        pl.semaphore_signal(barrier, inc=1, device_id={"dap": target}, device_id_type=MESH)


def met(place):
    pl.semaphore_wait(pltpu.get_barrier_semaphore(), len(place.partners))


class Gather:
    def __init__(self, place, out, sems):
        self.place, self.out, self.sems = place, out, sems
        self.sends = []

    def copy(self, kind, slot, block, target):
        return pltpu.make_async_remote_copy(
            src_ref=self.out.at[block],
            dst_ref=self.out.at[block],
            send_sem=self.sems[2 * kind].at[slot],
            recv_sem=self.sems[2 * kind + 1].at[slot],
            device_id={"dap": target},
            device_id_type=MESH,
        )

    def send(self, kind, slot, block, target):
        copy = self.copy(kind, slot, block, target)
        copy.start()
        self.sends.append(copy)

    def to_z(self, slot, block, target):
        self.send(0, slot, block, target)

    def to_f(self, d):
        p = self.place
        self.send(1, d, p.layer(p.me, d), p.f(p.me))

    def to_g(self, d, second):
        p = self.place
        block = p.layer(p.f(p.me) if second else p.me, d)
        self.send(2, d + 4 * second, block, p.g(p.me))

    def to_core(self, d, kind):
        p = self.place
        self.send(3, d + 4 * kind, self.mine(d, kind), flip(p.me, 1))

    def mine(self, d, kind):
        p = self.place
        b = p.me
        if kind % 2:
            b = p.f(b)
        if kind >= 2:
            b = p.g(b)
        return p.layer(b, d)

    def theirs(self, d, kind):
        p = self.place
        b = flip(p.me, 1)
        if kind % 2:
            b = p.g(b)
        if kind >= 2:
            b = p.f(b)
        return p.layer(b, d)

    def got(self, kind, slot, block):
        self.copy(kind, slot, block, flip(self.place.me, 1)).wait_recv()

    def start(self):
        p = self.place
        self.to_z(0, p.me, p.far)
        self.to_z(1, p.me, p.near)
        self.layer_out(0)

    def layer_out(self, d):
        self.to_f(d)
        self.to_g(d, 0)
        self.to_core(d, 0)

    def from_f(self, d):
        self.got(1, d, self.mine(d, 1))
        self.to_g(d, 1)
        self.to_core(d, 1)

    def from_g(self, d):
        self.got(2, d, self.mine(d, 2))
        self.to_core(d, 2)
        self.got(2, d + 4, self.mine(d, 3))
        self.to_core(d, 3)

    def steps(self):
        p = self.place
        self.got(0, 0, p.far)
        self.to_z(2, p.far, p.near)
        self.layer_out(1)
        yield
        self.got(0, 1, p.near)
        self.layer_out(2)
        self.from_f(0)
        yield
        self.got(0, 2, flip(p.near, 16))
        self.layer_out(3)
        self.from_f(1)
        yield
        self.from_f(2)
        self.from_g(0)
        yield
        self.from_f(3)
        self.from_g(1)
        yield
        self.from_g(2)
        yield
        self.from_g(3)
        yield

    def finish(self):
        for kind in range(4):
            for d in range(4):
                self.got(3, d + 4 * kind, self.theirs(d, kind))

    def sent(self):
        for copy in self.sends:
            copy.wait_send()


GATHER = (3, 3, 4, 4, 8, 8, 16, 16)


def gather_sems():
    return [pltpu.SemaphoreType.DMA((size,)) for size in GATHER]


class Exchange:
    def __init__(self, n, me, src, dst, piece, send, recv):
        self.n, self.me, self.src, self.dst = n, me, src, dst
        self.rows, self.first = pl.ds(piece * 16, 16), piece * n
        self.send, self.recv = send, recv

    def copy(self, k, block_out, block_in):
        return pltpu.make_async_remote_copy(
            src_ref=self.src.at[block_out, self.rows],
            dst_ref=self.dst.at[block_in, self.rows],
            send_sem=self.send.at[self.first + k],
            recv_sem=self.recv.at[self.first + k],
            device_id={"dap": block_out},
            device_id_type=MESH,
        )

    def start(self):
        def one(k, carry):
            self.copy(k, lax.rem(self.me + k, self.n), self.me).start()
            return carry

        lax.fori_loop(1, self.n, one, 0)
        self.dst[self.me, self.rows] = self.src[self.me, self.rows]

    def finish(self):
        def one(k, carry):
            target = lax.rem(self.me + k, self.n)
            self.copy(k, target, lax.rem(self.me + self.n - k, self.n)).wait_recv()
            return carry

        lax.fori_loop(1, self.n, one, 0)

    def sent(self):
        def one(k, carry):
            self.copy(k, lax.rem(self.me + k, self.n), self.me).wait_send()
            return carry

        lax.fori_loop(1, self.n, one, 0)


def iotas(rows, columns):
    shape = (rows, columns)
    return lax.broadcasted_iota(jnp.int32, shape, 0), lax.broadcasted_iota(jnp.int32, shape, 1)


def ones_where(condition):
    return condition.astype(full).astype(narrow)


def softmax(scores):
    powers = jnp.exp2(scores - jnp.max(scores, axis=-1, keepdims=True))
    return (powers * (1.0 / jnp.sum(powers, axis=-1, keepdims=True))).astype(narrow)


def attend(joint, gated, keeps, width):
    queries, keys_all = joint[:, :width], joint[:, width:]
    values_all, gates = gated[:, :width], gated[:, width:]
    groups = len(keeps)
    length = joint.shape[0] // groups
    lanes = lax.broadcasted_iota(jnp.int32, (1, width), 1) // HEAD
    totals = [None] * groups
    for h in range(HEADS):
        mine = ones_where(lanes == h)
        asked, given = queries * mine, values_all * mine
        for g in range(groups):
            part = slice(g * length, (g + 1) * length)
            scores = dot_nt(asked[part], keys_all[part]) * SCALE
            weights = softmax(jnp.where(keeps[g], scores, MASKED))
            mixed = dot(weights, given[part])
            totals[g] = mixed if totals[g] is None else totals[g] + mixed
    total = jnp.concatenate(totals, axis=0)
    return (total * jax.nn.sigmoid(gates.astype(full))).astype(narrow)


N_IN = 17


def kernel(n, *refs):
    inputs, (new_alignment, new_pair), scratch = refs[:N_IN], refs[N_IN : N_IN + 2], refs[N_IN + 2 :]
    held, scratch = scratch[:N_IN], scratch[N_IN:]
    (
        bias_a, bias_b, wide_bias, joints, asked_all, gate_all, mixed_all, residual, spread_a,
        spread_b, back_a, back_b, sent, columns, new_sent, back, left, right_a, right_b,
        wide_right, products, wide_output, turned_output, in_sems,
        to_send, to_recv, back_send, back_recv, *sems,
    ) = scratch
    (
        alignment, pair_rep, align_mask, residue_mask, row_gain, pair_gain, row_bias, row_scoring,
        row_values, row_output, column_gain, column_scoring, column_values, column_output,
        outer_gain, outer_inputs, outer_output,
    ) = held
    me = lax.axis_index("dap")
    place = Place(me)
    seqs, total_res, width = alignment.shape
    rows = pair_rep.shape[0]
    channels = pair_rep.shape[2]
    total_seqs = seqs * n
    half = rows // 2
    block = seqs * half

    order = (1, 5, 6, 2, 0, 4, 7, 8, 3, 9, 10, 11, 12, 13, 14, 15, 16)
    loads = [pltpu.make_async_copy(inputs[k], held[k], in_sems.at[k]) for k in range(N_IN)]
    for k in order:
        loads[k].start()
    greet(place)

    for k in (1, 5, 6, 2):
        loads[k].wait()
    biases = []
    for i in range(rows):
        normed = norm(pair_rep[i].astype(full), pair_gain[...])
        biases.append(dot_nt(row_bias[...], normed))
    biases = jnp.concatenate(biases, axis=0).astype(narrow)
    r, c = iotas(rows * HEADS, rows * HEADS)
    piece_of, rest = r // (half * HEADS), r % (half * HEADS)
    biases = dot(ones_where(c == (piece_of * half + rest % half) * HEADS + rest // half), biases).astype(narrow)
    bias_a[me] = biases[: half * HEADS]
    bias_b[me, : half * HEADS] = biases[half * HEADS :]
    mask_rows = jnp.concatenate([align_mask[...].astype(full), jnp.zeros((16 - seqs, total_res), full)], axis=0)
    bias_b[me, half * HEADS :] = mask_rows.astype(narrow)
    met(place)
    gather_a = Gather(place, bias_a, sems[:8])
    gather_b = Gather(place, bias_b, sems[8:16])
    gather_a.start()
    gather_b.start()
    steps_a, steps_b = gather_a.steps(), gather_b.steps()

    for k in (0, 4, 7, 8):
        loads[k].wait()
    r, c = iotas(total_res, total_res)
    lane_head = c // HEAD
    row_half = r % rows // half
    pair_masks = [ones_where(lane_head == 2 * hp + row_half) for hp in range(HEADS // 2)]
    doubles = [ones_where(c == r // rows * rows + piece * half + r % half) for piece in range(2)]

    def project(s):
        normed = norm(alignment[s].astype(full), row_gain[...])
        joint = dot(normed, row_scoring[...]).astype(narrow)
        gated = dot(normed, row_values[...]).astype(narrow)
        joints[s, :, :width] = joint[:, width:]
        joints[s, :, width:] = gated[:, :width]
        for piece in range(2):
            asked_all[piece, s] = dot(doubles[piece], joint[:, :width]).astype(narrow)
            gate_all[piece, s] = jax.nn.sigmoid(dot(doubles[piece], gated[:, width:]))

    for s in range(seqs):
        project(s)
        next(steps_a, None)
        if s > 0:
            next(steps_b, None)
    for k in (3, 9, 10, 11, 12, 13, 14, 15, 16):
        loads[k].wait()

    r, c = iotas(n * block, seqs * total_res)
    same = (r % block // half == c // total_res) & (r // block == c % total_res // rows) & (r % half == c % half)
    spread_a[...] = ones_where(same & (c % rows < half))
    spread_b[...] = ones_where(same & (c % rows >= half))
    spreads = (spread_a, spread_b)
    next(steps_a, None)
    next(steps_b, None)
    flat_alignment = alignment[...].reshape(seqs * total_res, width)
    for piece in range(2):
        residual[piece] = dot(spreads[piece][...], flat_alignment)
    next(steps_a, None)
    next(steps_b, None)
    r, c = iotas(seqs * total_res, n * block)
    same = (c % block // half == r // total_res) & (c // block == r % total_res // rows) & (c % half == r % half)
    back_a[...] = ones_where(same & (r % rows < half))
    back_b[...] = ones_where(same & (r % rows >= half))
    for _ in steps_a:
        next(steps_b, None)

    wide_output[...] = outer_output[...].astype(full).reshape(wide_output.shape)
    for g in range(C_OPM // 8):
        for parity in range(2):
            block_of = [wide_output[:, 2 * (g * 4 + t) + parity, :] for t in range(4)]
            turned_output[parity * channels : (parity + 1) * channels, g * 128 : (g + 1) * 128] = (
                jnp.concatenate(block_of, axis=0).T.astype(narrow)
            )
    gather_a.finish()

    residue_float = residue_mask[...].astype(full)
    bias_blocks = (bias_a, bias_b)
    keeps = [align_mask[s : s + 1, :].astype(full) * residue_float > 0 for s in range(seqs)]

    def row_piece(piece, between):
        wide_bias[...] = bias_blocks[piece][:, : half * HEADS, :].astype(full) * LOG2E
        for s in range(seqs):
            keys_all, values_all = joints[s, :, :width], joints[s, :, width:]
            total = None
            for hp in range(HEADS // 2):
                asked = asked_all[piece, s] * pair_masks[hp]
                bias = wide_bias[:, hp * rows : (hp + 1) * rows, :].reshape(total_res, total_res)
                scores = dot_nt(asked, keys_all) * SCALE + bias
                weights = softmax(jnp.where(keeps[s], scores, MASKED))
                mixed = dot(weights, values_all) * pair_masks[hp].astype(full)
                total = mixed if total is None else total + mixed
            mixed_all[s * total_res : (s + 1) * total_res, :] = (total * gate_all[piece, s]).astype(narrow)
            between()
        mixed = dot(spread_a[...], mixed_all[...]) + dot(spread_b[...], mixed_all[...])
        updated = residual[piece] + dot(mixed.astype(narrow), row_output[...])
        sent[:, piece * block : (piece + 1) * block, :] = updated.astype(narrow).reshape(n, block, width)
        exchange = Exchange(n, me, sent, columns, piece, to_send, to_recv)
        exchange.start()
        return exchange

    def relay_b():
        next(steps_b, None)
        next(steps_b, None)

    to_a = row_piece(0, relay_b)
    for _ in steps_b:
        pass
    gather_b.finish()
    to_b = row_piece(1, lambda: None)

    every_mask = bias_b[:, half * HEADS :, :].reshape(n * 16, total_res)
    r, c = iotas(total_seqs, n * 16)
    mask = dot(ones_where(c == r // seqs * 16 + r % seqs), every_mask).astype(narrow)
    r, c = iotas(rows, total_res)
    own = ones_where(c == me * rows + r)
    keep_columns = dot_nt(own, mask)
    row_factor = jnp.sum(own.astype(full) * residue_float, axis=-1, keepdims=True)
    pair_count = dot(keep_columns.astype(narrow), mask)
    scale = row_factor * residue_float / (0.001 + pair_count)

    length = half * total_seqs
    r, c = iotas(length, length)
    into = ones_where(c == r % total_seqs * half + r // total_seqs)
    out_of = ones_where(r == c % total_seqs * half + c // total_seqs)
    r, c = iotas(C_OPM * half, C_OPM * half)
    by_channel = ones_where(c == r % half * C_OPM + r // half)
    rights = (right_a, right_b)

    def column_piece(piece):
        rows_here = pl.ds(piece * block, block)
        stream = dot(into, columns[:, rows_here].reshape(length, width))
        normed = norm(stream, column_gain[...])
        joint = dot(normed, column_scoring[...]).astype(narrow)
        gated = dot(normed, column_values[...]).astype(narrow)
        mine = range(piece * half, (piece + 1) * half)
        mixed = attend(joint, gated, [keep_columns[i : i + 1, :] > 0 for i in mine], width)
        second = (stream + dot(mixed, column_output[...])).astype(narrow)
        outer_normed = norm(second.astype(full), outer_gain[...])
        right = []
        for t, i in enumerate(mine):
            part = slice(t * total_seqs, (t + 1) * total_seqs)
            sides = dot_nt(outer_inputs[...], outer_normed[part]) * keep_columns[i : i + 1, :]
            left[i] = sides[:C_OPM].astype(narrow)
            right.append(sides[C_OPM:].astype(narrow))
        rights[piece][me] = dot(by_channel, jnp.concatenate(right, axis=0)).astype(narrow)
        gather = Gather(place, rights[piece], sems[16 + 8 * piece : 24 + 8 * piece])
        gather.start()
        new_sent[:, rows_here] = dot(out_of, second).astype(narrow).reshape(n, block, width)
        exchange = Exchange(n, me, new_sent, back, piece, back_send, back_recv)
        exchange.start()
        return gather, exchange

    to_a.finish()
    right_a_gather, home_a = column_piece(0)
    steps_a = right_a_gather.steps()
    for _ in steps_a:
        pass
    to_b.finish()
    right_b_gather, home_b = column_piece(1)
    right_a_gather.finish()
    steps_b = right_b_gather.steps()

    sides = left[...].reshape(rows * C_OPM, total_seqs)

    def outer(piece):
        wide_right[...] = rights[piece][...].astype(full)
        for e in range(C_OPM // 2):
            some = wide_right[:, e * rows : (e + 1) * rows, :].reshape(total_res, total_seqs)
            product = dot_nt(sides, some.astype(narrow)).astype(narrow)
            products[piece, :, e * C_OPM : (e + 1) * C_OPM, :] = product.reshape(rows, C_OPM, total_res)

    next(steps_b, None)
    next(steps_b, None)
    next(steps_b, None)
    outer(0)
    for _ in steps_b:
        pass
    home_a.finish()
    flat_a = dot(back_a[...], back[:, :block].reshape(n * block, width))
    new_alignment[...] = flat_a.astype(narrow).reshape(new_alignment.shape)
    right_b_gather.finish()
    outer(1)
    low = lax.broadcasted_iota(jnp.int32, (1, total_res), 1) % rows < half
    for i in range(rows):
        first = dot(turned_output[...], products[0, i])
        second = dot(turned_output[...], products[1, i])
        kept = jnp.where(low, first[:channels], second[channels:])
        moved = jnp.where(
            low,
            pltpu.roll(first[channels:], total_res - half, 1),
            pltpu.roll(second[:channels], half, 1),
        )
        flat = (kept + moved) * scale[i : i + 1, :]
        new_pair[i] = (pair_rep[i].astype(full) + flat.T).astype(narrow)
    home_b.finish()
    flat_b = dot(back_b[...], back[:, block:].reshape(n * block, width))
    new_alignment[...] = (new_alignment[...].astype(full) + flat_b.reshape(new_alignment.shape)).astype(narrow)
    for exchange in (to_a, to_b, home_a, home_b):
        exchange.sent()
    for gather in (gather_a, gather_b, right_a_gather, right_b_gather):
        gather.sent()


def body(n, alignment, pair_rep, align_mask, residue_mask, *rest):
    (
        row_gain, pair_gain, row_bias, row_scoring, row_values, row_output, column_gain,
        column_scoring, column_values, column_output, outer_gain, outer_inputs, outer_output,
    ) = rest
    seqs, total_res, width = alignment.shape
    rows, _, channels = pair_rep.shape
    total_seqs = seqs * n
    half = rows // 2
    arguments = (
        alignment, pair_rep, align_mask, residue_mask[None], row_gain[None], pair_gain[None],
        row_bias.T, row_scoring, row_values, row_output, column_gain[None], column_scoring,
        column_values, column_output, outer_gain[None], outer_inputs.T, outer_output,
    )
    dma = pltpu.SemaphoreType.DMA
    blocks = (n, seqs * rows, width)
    sent = n * seqs * half
    right_shape = (n, C_OPM * half, total_seqs)
    return pl.pallas_call(
        functools.partial(kernel, n),
        out_shape=(
            jax.ShapeDtypeStruct(alignment.shape, narrow),
            jax.ShapeDtypeStruct(pair_rep.shape, narrow),
        ),
        in_specs=[pl.BlockSpec(memory_space=pltpu.HBM)] * N_IN,
        out_specs=(VMEM, VMEM),
        scratch_shapes=[pltpu.VMEM(array.shape, array.dtype) for array in arguments]
        + [
            pltpu.VMEM((n, HEADS * half, total_res), narrow),
            pltpu.VMEM((n, HEADS * half + 16, total_res), narrow),
            pltpu.VMEM((n, HEADS * half, total_res), full),
            pltpu.VMEM((seqs, total_res, 2 * width), narrow),
            pltpu.VMEM((2, seqs, total_res, width), narrow),
            pltpu.VMEM((2, seqs, total_res, width), full),
            pltpu.VMEM((seqs * total_res, width), narrow),
            pltpu.VMEM((2, sent, width), full),
            pltpu.VMEM((sent, seqs * total_res), narrow),
            pltpu.VMEM((sent, seqs * total_res), narrow),
            pltpu.VMEM((seqs * total_res, sent), narrow),
            pltpu.VMEM((seqs * total_res, sent), narrow),
            pltpu.VMEM(blocks, narrow),
            pltpu.VMEM(blocks, narrow),
            pltpu.VMEM(blocks, narrow),
            pltpu.VMEM(blocks, narrow),
            pltpu.VMEM((rows, C_OPM, total_seqs), narrow),
            pltpu.VMEM(right_shape, narrow),
            pltpu.VMEM(right_shape, narrow),
            pltpu.VMEM(right_shape, full),
            pltpu.VMEM((2, rows, C_OPM * C_OPM // 2, total_res), narrow),
            pltpu.VMEM((C_OPM, C_OPM, channels), full),
            pltpu.VMEM((2 * channels, C_OPM * C_OPM // 2), narrow),
            dma((N_IN,)),
        ]
        + [dma((2 * n,))] * 4
        + gather_sems() * 4,
        compiler_params=pltpu.CompilerParams(
            vmem_limit_bytes=LIMIT, collective_id=0, has_side_effects=True
        ),
        name="evoformer",
    )(*arguments)


def solution(mesh):
    split = P(("dp", "dap"), None, None)
    in_specs = (split, split, P(("dp", "dap"), None), P("dp")) + (P(),) * 13
    return jax.shard_map(
        functools.partial(body, mesh.shape["dap"]),
        mesh=mesh,
        in_specs=in_specs,
        out_specs=(split, split),
        check_vma=False,
    )
```

```python
import functools
import math

import jax
import jax.numpy as jnp
from jax import lax
from jax.experimental import pallas as pl
from jax.experimental.pallas import tpu as pltpu
from jax.sharding import PartitionSpec as P

HEADS = 8
HEAD = 32
C_OPM = 32
LOG2E = math.log2(math.e)
SCALE = LOG2E / math.sqrt(HEAD)
MASKED = -1000000000.0 * LOG2E
NT = (((1,), (1,)), ((), ()))
MESH = pl.DeviceIdType.MESH
VMEM = pl.BlockSpec(memory_space=pltpu.VMEM)
LIMIT = 60 * 1024 * 1024
narrow, full = jnp.bfloat16, jnp.float32


def norm(wide, gain):
    average = jnp.mean(wide, axis=-1, keepdims=True)
    centred = wide - average
    spread = jnp.mean(centred * centred, axis=-1, keepdims=True)
    return (centred * lax.rsqrt(spread + 1e-05) * gain).astype(narrow)


def dot(a, b):
    return jnp.dot(a, b, preferred_element_type=full)


def dot_nt(a, b):
    return lax.dot_general(a, b, NT, preferred_element_type=full)


def flip(b, bit):
    return b + bit - 2 * bit * lax.rem(b // bit, 2)


class Place:
    def __init__(self, me):
        self.me, self.other, self.core = me, flip(me, 1), lax.rem(me, 2)
        self.partners = [self.layer(me, d) for d in (1, 2, 3)] + [self.plane(me, k) for k in (1, 2, 3)] + [self.other]

    def plane(self, b, k):
        if k % 2:
            b = flip(b, 2)
        return flip(b, 4) if k >= 2 else b

    def turn(self, b, k, core):
        x, y = flip(b, 2) - b, flip(b, 4) - b
        if k % 2:
            b = b + (1 - core) * x + core * y
        return b + core * x + (1 - core) * y if k >= 2 else b

    def layer(self, b, d):
        if d % 2:
            b = flip(b, 16)
        return flip(b, 8) if d >= 2 else b


def greet(place):
    barrier = pltpu.get_barrier_semaphore()
    for target in place.partners:
        pl.semaphore_signal(barrier, inc=1, device_id={"dap": target}, device_id_type=MESH)


def met(place):
    pl.semaphore_wait(pltpu.get_barrier_semaphore(), len(place.partners))


class Gather:
    def __init__(self, place, out, sems, z_relay, p_relay):
        self.place, self.out, self.sems = place, out, sems
        self.z_relay, self.p_relay = z_relay, p_relay
        self.sends = []

    def copy(self, kind, slot, block, target):
        return pltpu.make_async_remote_copy(
            src_ref=self.out.at[block],
            dst_ref=self.out.at[block],
            send_sem=self.sems[2 * kind].at[slot],
            recv_sem=self.sems[2 * kind + 1].at[slot],
            device_id={"dap": target},
            device_id_type=MESH,
        )

    def send(self, kind, slot, block, target):
        copy = self.copy(kind, slot, block, target)
        copy.start()
        self.sends.append(copy)

    def got(self, kind, slot, block):
        self.copy(kind, slot, block, self.place.other).wait_recv()

    def mine(self, d, k):
        return self.place.layer(self.spot(self.place.me, k, self.place.core), d)

    def theirs(self, d, k):
        return self.place.layer(self.spot(self.place.other, k, 1 - self.place.core), d)

    def spot(self, b, k, core):
        return self.place.turn(b, k, core) if self.p_relay else self.place.plane(b, k)

    def layer_out(self, d):
        p = self.place
        for k in (1, 2) if self.p_relay else (1, 2, 3):
            self.send(1, d * 4 + k, self.mine(d, 0), self.mine(0, k))
        self.send(2, d * 4, self.mine(d, 0), p.other)

    def from_plane(self, d, ks=(1, 2, 3)):
        for k in ks:
            self.got(1, d * 4 + k, self.mine(d, k))
            if self.p_relay and k == 1:
                self.send(1, d * 4 + 3, self.mine(d, 1), self.mine(0, 2))
            self.send(2, d * 4 + k, self.mine(d, k), self.place.other)

    def start(self):
        p = self.place
        for d in (1, 2) if self.z_relay else (1, 3, 2):
            self.send(0, d, p.me, p.layer(p.me, d))
        self.layer_out(0)

    def steps(self):
        p = self.place
        if self.z_relay:
            self.got(0, 1, self.mine(1, 0))
            self.send(0, 3, self.mine(1, 0), p.layer(p.me, 2))
            self.layer_out(1)
            yield
        self.got(0, 2, self.mine(2, 0))
        self.layer_out(2)
        yield
        if not self.z_relay:
            self.got(0, 1, self.mine(1, 0))
            self.layer_out(1)
            yield
        self.got(0, 3, self.mine(3, 0))
        self.layer_out(3)
        yield
        if self.p_relay:
            for d in (0, 1, 2, 3):
                self.from_plane(d, (1,))
            yield
            for d in (0, 1, 2, 3):
                self.from_plane(d, (2, 3))
                yield
        else:
            for d in (0, 2, 1, 3):
                self.from_plane(d)
                yield

    def finish(self):
        for d in range(4):
            for k in range(4):
                self.got(2, d * 4 + k, self.theirs(d, k))

    def sent(self):
        for copy in self.sends:
            copy.wait_send()


def gather_sems():
    return [pltpu.SemaphoreType.DMA((size,)) for size in (4, 4, 16, 16, 16, 16)]


class Exchange:
    def __init__(self, n, me, src, dst, piece, send, recv):
        self.n, self.me, self.src, self.dst = n, me, src, dst
        self.rows, self.first = pl.ds(piece * 16, 16), piece * n
        self.send, self.recv = send, recv

    def copy(self, k, block_out, block_in):
        return pltpu.make_async_remote_copy(
            src_ref=self.src.at[block_out, self.rows],
            dst_ref=self.dst.at[block_in, self.rows],
            send_sem=self.send.at[self.first + k],
            recv_sem=self.recv.at[self.first + k],
            device_id={"dap": block_out},
            device_id_type=MESH,
        )

    def start(self):
        def one(k, carry):
            self.copy(k, lax.rem(self.me + k, self.n), self.me).start()
            return carry

        lax.fori_loop(1, self.n, one, 0)
        self.dst[self.me, self.rows] = self.src[self.me, self.rows]

    def finish(self):
        def one(k, carry):
            target = lax.rem(self.me + k, self.n)
            self.copy(k, target, lax.rem(self.me + self.n - k, self.n)).wait_recv()
            return carry

        lax.fori_loop(1, self.n, one, 0)

    def sent(self):
        def one(k, carry):
            self.copy(k, lax.rem(self.me + k, self.n), self.me).wait_send()
            return carry

        lax.fori_loop(1, self.n, one, 0)


def iotas(rows, columns):
    shape = (rows, columns)
    return lax.broadcasted_iota(jnp.int32, shape, 0), lax.broadcasted_iota(jnp.int32, shape, 1)


def ones_where(condition):
    return condition.astype(full).astype(narrow)


def softmax(scores):
    powers = jnp.exp2(scores - jnp.max(scores, axis=-1, keepdims=True))
    return (powers * (1.0 / jnp.sum(powers, axis=-1, keepdims=True))).astype(narrow)


def attend(joint, gated, keeps, width, between):
    groups = len(keeps)
    length = joint.shape[0] // groups
    side = width // 2
    some = HEADS // 2
    lanes = lax.broadcasted_iota(jnp.int32, (length, side), 1) // HEAD
    picks = [ones_where(lanes == h) for h in range(some)]
    totals = []
    for g in range(groups):
        part = slice(g * length, (g + 1) * length)
        sides = []
        for first in (0, side):
            queries, keys_all = joint[part, first : first + side], joint[part, width + first : width + first + side]
            asked = jnp.concatenate([queries * pick for pick in picks], axis=0)
            scores = dot_nt(asked, keys_all) * SCALE
            weights = softmax(jnp.where(keeps[g], scores, MASKED))
            mixed = dot(weights, gated[part, first : first + side])
            total = mixed[:length]
            for h in range(1, some):
                total = jnp.where(lanes == h, mixed[h * length : (h + 1) * length], total)
            sides.append(total)
            between()
        totals.append(jnp.concatenate(sides, axis=1))
    total = jnp.concatenate(totals, axis=0)
    return (total * jax.nn.sigmoid(gated[:, width:].astype(full))).astype(narrow)


N_IN = 17


def kernel(n, *refs):
    inputs, (new_alignment, new_pair), scratch = refs[:N_IN], refs[N_IN : N_IN + 2], refs[N_IN + 2 :]
    held, scratch = scratch[:N_IN], scratch[N_IN:]
    (
        bias_a, bias_b, wide_bias, joints, asked_all, gate_all, mixed_all, residual, spread_a,
        spread_b, spread_both, back_a, back_b, sent, columns, new_sent, back, left, right_a, right_b,
        wide_right, products, outer_a, wide_output, turned_output, in_sems,
        to_send, to_recv, back_send, back_recv, *sems,
    ) = scratch
    (
        alignment, pair_rep, align_mask, residue_mask, row_gain, pair_gain, row_bias, row_scoring,
        row_values, row_output, column_gain, column_scoring, column_values, column_output,
        outer_gain, outer_inputs, outer_output,
    ) = held
    me = lax.axis_index("dap")
    place = Place(me)
    seqs, total_res, width = alignment.shape
    rows = pair_rep.shape[0]
    channels = pair_rep.shape[2]
    total_seqs = seqs * n
    half = rows // 2
    block = seqs * half

    order = (1, 5, 6, 2, 0, 4, 7, 8, 3, 9, 10, 11, 12, 13, 14, 15, 16)
    loads = [pltpu.make_async_copy(inputs[k], held[k], in_sems.at[k]) for k in range(N_IN)]
    for k in order:
        loads[k].start()
    greet(place)

    for k in (1, 5, 6, 2):
        loads[k].wait()
    biases = []
    for i in range(rows):
        normed = norm(pair_rep[i].astype(full), pair_gain[...])
        biases.append(dot_nt(row_bias[...], normed))
    biases = jnp.concatenate(biases, axis=0).astype(narrow)
    r, c = iotas(rows * HEADS, rows * HEADS)
    piece_of, rest = r // (half * HEADS), r % (half * HEADS)
    biases = dot(ones_where(c == (piece_of * half + rest % half) * HEADS + rest // half), biases).astype(narrow)
    bias_a[me] = biases[: half * HEADS]
    bias_b[me, : half * HEADS] = biases[half * HEADS :]
    mask_rows = jnp.concatenate([align_mask[...].astype(full), jnp.zeros((16 - seqs, total_res), full)], axis=0)
    bias_b[me, half * HEADS :] = mask_rows.astype(narrow)
    met(place)
    gather_a = Gather(place, bias_a, sems[:6], False, False)
    gather_b = Gather(place, bias_b, sems[6:12], False, False)
    gather_a.start()
    steps_a, steps_b = gather_a.steps(), gather_b.steps()

    for k in (0, 4, 7, 8):
        loads[k].wait()
    r, c = iotas(total_res, total_res)
    lane_head = c[:, : width // 2] // HEAD
    row_half = r[:, : width // 2] % rows // half
    kept = [lane_head == 2 * hp + row_half for hp in range(2)]
    pair_masks = [ones_where(k) for k in kept]
    doubles = [ones_where(c == r // rows * rows + piece * half + r % half) for piece in range(2)]

    def project(s):
        normed = norm(alignment[s].astype(full), row_gain[...])
        joint = dot(normed, row_scoring[...]).astype(narrow)
        gated = dot(normed, row_values[...]).astype(narrow)
        joints[s, :, :width] = joint[:, width:]
        joints[s, :, width:] = gated[:, :width]
        for piece in range(2):
            asked_all[piece, s] = dot(doubles[piece], joint[:, :width]).astype(narrow)
            gate_all[piece, s] = jax.nn.sigmoid(dot(doubles[piece], gated[:, width:]))

    for s in range(seqs):
        project(s)
        if s == 1:
            for _ in range(3):
                next(steps_a, None)
            gather_b.start()
    for k in (3, 9, 10, 11, 12, 13, 14, 15, 16):
        loads[k].wait()

    r, c = iotas(n * block, seqs * total_res)
    same = (r % block // half == c // total_res) & (r // block == c % total_res // rows) & (r % half == c % half)
    spread_a[...] = ones_where(same & (c % rows < half))
    spread_b[...] = ones_where(same & (c % rows >= half))
    spread_both[...] = ones_where(same)
    spreads = (spread_a, spread_b)
    next(steps_a, None)
    next(steps_a, None)
    for _ in range(3):
        next(steps_b, None)
    flat_alignment = alignment[...].reshape(seqs * total_res, width)
    for piece in range(2):
        residual[piece] = dot(spreads[piece][...], flat_alignment)
    next(steps_a, None)
    r, c = iotas(seqs * total_res, n * block)
    same = (c % block // half == r // total_res) & (c // block == r % total_res // rows) & (c % half == r % half)
    back_a[...] = ones_where(same & (r % rows < half))
    back_b[...] = ones_where(same & (r % rows >= half))
    for _ in steps_a:
        pass

    wide_output[...] = outer_output[...].astype(full).reshape(wide_output.shape)
    for g in range(C_OPM // 8):
        for parity in range(2):
            block_of = [wide_output[:, 2 * (g * 4 + t) + parity, :] for t in range(4)]
            turned_output[parity * channels : (parity + 1) * channels, g * 128 : (g + 1) * 128] = (
                jnp.concatenate(block_of, axis=0).T.astype(narrow)
            )
    gather_a.finish()

    residue_float = residue_mask[...].astype(full)
    bias_blocks = (bias_a, bias_b)
    keeps = [align_mask[s : s + 1, :].astype(full) * residue_float > 0 for s in range(seqs)]

    def row_piece(piece, between):
        wide_bias[...] = bias_blocks[piece][:, : half * HEADS, :].astype(full) * LOG2E
        for s in range(seqs):
            keys_all, values_all = joints[s, :, :width], joints[s, :, width:]
            side = width // 2
            sides = []
            for hp in range(HEADS // 2):
                lanes_here = slice(hp // 2 * side, (hp // 2 + 1) * side)
                asked = asked_all[piece, s][:, lanes_here] * pair_masks[hp % 2]
                bias = wide_bias[:, hp * rows : (hp + 1) * rows, :].reshape(total_res, total_res)
                scores = dot_nt(asked, keys_all[:, lanes_here]) * SCALE + bias
                weights = softmax(jnp.where(keeps[s], scores, MASKED))
                mixed = dot(weights, values_all[:, lanes_here])
                if hp % 2:
                    sides[-1] = jnp.where(kept[1], mixed, sides[-1])
                else:
                    sides.append(jnp.where(kept[0], mixed, 0.0))
            total = jnp.concatenate(sides, axis=1)
            mixed_all[s * total_res : (s + 1) * total_res, :] = (total * gate_all[piece, s]).astype(narrow)
            between()
        mixed = dot(spread_both[...], mixed_all[...])
        updated = residual[piece] + dot(mixed.astype(narrow), row_output[...])
        sent[:, piece * block : (piece + 1) * block, :] = updated.astype(narrow).reshape(n, block, width)
        exchange = Exchange(n, me, sent, columns, piece, to_send, to_recv)
        exchange.start()
        return exchange

    def relay_b():
        next(steps_b, None)

    to_a = row_piece(0, relay_b)
    for _ in steps_b:
        pass
    gather_b.finish()
    to_b = row_piece(1, lambda: None)

    every_mask = bias_b[:, half * HEADS :, :].reshape(n * 16, total_res)
    r, c = iotas(total_seqs, n * 16)
    mask = dot(ones_where(c == r // seqs * 16 + r % seqs), every_mask).astype(narrow)
    r, c = iotas(rows, total_res)
    own = ones_where(c == me * rows + r)
    keep_columns = dot_nt(own, mask)
    row_factor = jnp.sum(own.astype(full) * residue_float, axis=-1, keepdims=True)
    pair_count = dot(keep_columns.astype(narrow), mask)
    scale = row_factor * residue_float / (0.001 + pair_count)

    length = half * total_seqs
    r, c = iotas(length, length)
    into = ones_where(c == r % total_seqs * half + r // total_seqs)
    out_of = ones_where(r == c % total_seqs * half + c // total_seqs)
    r, c = iotas(C_OPM * half, C_OPM * half)
    by_channel = ones_where(c == r % half * C_OPM + r // half)
    rights = (right_a, right_b)

    def column_piece(piece, between):
        rows_here = pl.ds(piece * block, block)
        stream = dot(into, columns[:, rows_here].reshape(length, width))
        normed = norm(stream, column_gain[...])
        joint = dot(normed, column_scoring[...]).astype(narrow)
        gated = dot(normed, column_values[...]).astype(narrow)
        mine = range(piece * half, (piece + 1) * half)
        mixed = attend(joint, gated, [keep_columns[i : i + 1, :] > 0 for i in mine], width, between)
        second = (stream + dot(mixed, column_output[...])).astype(narrow)
        outer_normed = norm(second.astype(full), outer_gain[...])
        right = []
        for t, i in enumerate(mine):
            part = slice(t * total_seqs, (t + 1) * total_seqs)
            sides = dot_nt(outer_inputs[...], outer_normed[part]) * keep_columns[i : i + 1, :]
            left[i] = sides[:C_OPM].astype(narrow)
            right.append(sides[C_OPM:].astype(narrow))
        rights[piece][me] = dot(by_channel, jnp.concatenate(right, axis=0)).astype(narrow)
        gather = Gather(place, rights[piece], sems[12 + 6 * piece : 18 + 6 * piece], False, False)
        gather.start()
        new_sent[:, rows_here] = dot(out_of, second).astype(narrow).reshape(n, block, width)
        steps = gather.steps()
        for _ in range(3):
            next(steps, None)
        exchange = Exchange(n, me, new_sent, back, piece, back_send, back_recv)
        exchange.start()
        return gather, steps, exchange

    to_a.finish()
    right_a_gather, steps_a, home_a = column_piece(0, lambda: None)
    next(steps_a, None)
    to_b.finish()
    right_b_gather, steps_b, home_b = column_piece(1, lambda: None)
    for _ in steps_a:
        pass

    sides = left[...].reshape(rows * C_OPM, total_seqs)

    def outer(piece):
        wide_right[...] = rights[piece][...].astype(full)
        for e in range(C_OPM // 2):
            some = wide_right[:, e * rows : (e + 1) * rows, :].reshape(total_res, total_seqs)
            product = dot_nt(sides, some.astype(narrow)).astype(narrow)
            products[:, e * C_OPM : (e + 1) * C_OPM, :] = product.reshape(rows, C_OPM, total_res)
        for i in range(rows):
            yield i, dot(turned_output[...], products[i])

    low = lax.broadcasted_iota(jnp.int32, (1, total_res), 1) % rows < half
    next(steps_b, None)
    right_a_gather.finish()
    for i, first in outer(0):
        moved = pltpu.roll(first[channels:], total_res - half, 1)
        outer_a[i] = jnp.where(low, first[:channels] + moved, 0.0)
        if i in (0, 2, 4, 6):
            next(steps_b, None)
    for _ in steps_b:
        pass
    home_a.finish()
    flat_a = dot(back_a[...], back[:, :block].reshape(n * block, width))
    new_alignment[...] = flat_a.astype(narrow).reshape(new_alignment.shape)
    right_b_gather.finish()
    for i, second in outer(1):
        moved = pltpu.roll(second[:channels], half, 1)
        flat = (outer_a[i] + jnp.where(low, 0.0, second[channels:] + moved)) * scale[i : i + 1, :]
        new_pair[i] = (pair_rep[i].astype(full) + flat.T).astype(narrow)
    home_b.finish()
    flat_b = dot(back_b[...], back[:, block:].reshape(n * block, width))
    new_alignment[...] = (new_alignment[...].astype(full) + flat_b.reshape(new_alignment.shape)).astype(narrow)
    for exchange in (to_a, to_b, home_a, home_b):
        exchange.sent()
    for gather in (gather_a, gather_b, right_a_gather, right_b_gather):
        gather.sent()


def body(n, alignment, pair_rep, align_mask, residue_mask, *rest):
    (
        row_gain, pair_gain, row_bias, row_scoring, row_values, row_output, column_gain,
        column_scoring, column_values, column_output, outer_gain, outer_inputs, outer_output,
    ) = rest
    seqs, total_res, width = alignment.shape
    rows, _, channels = pair_rep.shape
    total_seqs = seqs * n
    half = rows // 2
    arguments = (
        alignment, pair_rep, align_mask, residue_mask[None], row_gain[None], pair_gain[None],
        row_bias.T, row_scoring, row_values, row_output, column_gain[None], column_scoring,
        column_values, column_output, outer_gain[None], outer_inputs.T, outer_output,
    )
    dma = pltpu.SemaphoreType.DMA
    blocks = (n, seqs * rows, width)
    sent = n * seqs * half
    right_shape = (n, C_OPM * half, total_seqs)
    return pl.pallas_call(
        functools.partial(kernel, n),
        out_shape=(
            jax.ShapeDtypeStruct(alignment.shape, narrow),
            jax.ShapeDtypeStruct(pair_rep.shape, narrow),
        ),
        in_specs=[pl.BlockSpec(memory_space=pltpu.HBM)] * N_IN,
        out_specs=(VMEM, VMEM),
        scratch_shapes=[pltpu.VMEM(array.shape, array.dtype) for array in arguments]
        + [
            pltpu.VMEM((n, HEADS * half, total_res), narrow),
            pltpu.VMEM((n, HEADS * half + 16, total_res), narrow),
            pltpu.VMEM((n, HEADS * half, total_res), full),
            pltpu.VMEM((seqs, total_res, 2 * width), narrow),
            pltpu.VMEM((2, seqs, total_res, width), narrow),
            pltpu.VMEM((2, seqs, total_res, width), full),
            pltpu.VMEM((seqs * total_res, width), narrow),
            pltpu.VMEM((2, sent, width), full),
            pltpu.VMEM((sent, seqs * total_res), narrow),
            pltpu.VMEM((sent, seqs * total_res), narrow),
            pltpu.VMEM((sent, seqs * total_res), narrow),
            pltpu.VMEM((seqs * total_res, sent), narrow),
            pltpu.VMEM((seqs * total_res, sent), narrow),
            pltpu.VMEM(blocks, narrow),
            pltpu.VMEM(blocks, narrow),
            pltpu.VMEM(blocks, narrow),
            pltpu.VMEM(blocks, narrow),
            pltpu.VMEM((rows, C_OPM, total_seqs), narrow),
            pltpu.VMEM(right_shape, narrow),
            pltpu.VMEM(right_shape, narrow),
            pltpu.VMEM(right_shape, full),
            pltpu.VMEM((rows, C_OPM * C_OPM // 2, total_res), narrow),
            pltpu.VMEM((rows, channels, total_res), full),
            pltpu.VMEM((C_OPM, C_OPM, channels), full),
            pltpu.VMEM((2 * channels, C_OPM * C_OPM // 2), narrow),
            dma((N_IN,)),
        ]
        + [dma((2 * n,))] * 4
        + gather_sems() * 4,
        compiler_params=pltpu.CompilerParams(
            vmem_limit_bytes=LIMIT, collective_id=0, has_side_effects=True
        ),
        name="evoformer",
    )(*arguments)


def solution(mesh):
    split = P(("dp", "dap"), None, None)
    in_specs = (split, split, P(("dp", "dap"), None), P("dp")) + (P(),) * 13
    return jax.shard_map(
        functools.partial(body, mesh.shape["dap"]),
        mesh=mesh,
        in_specs=in_specs,
        out_specs=(split, split),
        check_vma=False,
    )
```

```python
import functools
import math

import jax
import jax.numpy as jnp
from jax import lax
from jax.experimental import pallas as pl
from jax.experimental.pallas import tpu as pltpu
from jax.sharding import PartitionSpec as P

HEADS = 8
HEAD = 32
C_OPM = 32
LOG2E = math.log2(math.e)
SCALE = LOG2E / math.sqrt(HEAD)
MASKED = -1000000000.0 * LOG2E
NT = (((1,), (1,)), ((), ()))
MESH = pl.DeviceIdType.MESH
VMEM = pl.BlockSpec(memory_space=pltpu.VMEM)
LIMIT = 60 * 1024 * 1024
narrow, full = jnp.bfloat16, jnp.float32


def norm(wide, gain):
    average = jnp.mean(wide, axis=-1, keepdims=True)
    centred = wide - average
    spread = jnp.mean(centred * centred, axis=-1, keepdims=True)
    return (centred * lax.rsqrt(spread + 1e-05) * gain).astype(narrow)


def dot(a, b):
    return jnp.dot(a, b, preferred_element_type=full)


def dot_nt(a, b):
    return lax.dot_general(a, b, NT, preferred_element_type=full)


def flip(b, bit):
    return b + bit - 2 * bit * lax.rem(b // bit, 2)


class Place:
    def __init__(self, me):
        self.me, self.other, self.core = me, flip(me, 1), lax.rem(me, 2)
        self.partners = [self.layer(me, d) for d in (1, 2, 3)] + [self.plane(me, k) for k in (1, 2, 3)] + [self.other]

    def plane(self, b, k):
        if k % 2:
            b = flip(b, 2)
        return flip(b, 4) if k >= 2 else b

    def turn(self, b, k, core):
        x, y = flip(b, 2) - b, flip(b, 4) - b
        if k % 2:
            b = b + (1 - core) * x + core * y
        return b + core * x + (1 - core) * y if k >= 2 else b

    def layer(self, b, d):
        if d % 2:
            b = flip(b, 16)
        return flip(b, 8) if d >= 2 else b


def greet(place):
    barrier = pltpu.get_barrier_semaphore()
    for target in place.partners:
        pl.semaphore_signal(barrier, inc=1, device_id={"dap": target}, device_id_type=MESH)


def met(place):
    pl.semaphore_wait(pltpu.get_barrier_semaphore(), len(place.partners))


class Gather:
    def __init__(self, place, out, sems, z_relay, p_relay):
        self.place, self.out, self.sems = place, out, sems
        self.z_relay, self.p_relay = z_relay, p_relay
        self.sends = []

    def copy(self, kind, slot, block, target):
        return pltpu.make_async_remote_copy(
            src_ref=self.out.at[block],
            dst_ref=self.out.at[block],
            send_sem=self.sems[2 * kind].at[slot],
            recv_sem=self.sems[2 * kind + 1].at[slot],
            device_id={"dap": target},
            device_id_type=MESH,
        )

    def send(self, kind, slot, block, target):
        copy = self.copy(kind, slot, block, target)
        copy.start()
        self.sends.append(copy)

    def got(self, kind, slot, block):
        self.copy(kind, slot, block, self.place.other).wait_recv()

    def mine(self, d, k):
        return self.place.layer(self.spot(self.place.me, k, self.place.core), d)

    def theirs(self, d, k):
        return self.place.layer(self.spot(self.place.other, k, 1 - self.place.core), d)

    def spot(self, b, k, core):
        return self.place.turn(b, k, core) if self.p_relay else self.place.plane(b, k)

    def layer_out(self, d):
        p = self.place
        for k in (1, 2) if self.p_relay else (1, 2, 3):
            self.send(1, d * 4 + k, self.mine(d, 0), self.mine(0, k))
        self.send(2, d * 4, self.mine(d, 0), p.other)

    def from_plane(self, d, ks=(1, 2, 3)):
        for k in ks:
            self.got(1, d * 4 + k, self.mine(d, k))
            if self.p_relay and k == 1:
                self.send(1, d * 4 + 3, self.mine(d, 1), self.mine(0, 2))
            self.send(2, d * 4 + k, self.mine(d, k), self.place.other)

    def start(self):
        p = self.place
        for d in (1, 2) if self.z_relay else (1, 3, 2):
            self.send(0, d, p.me, p.layer(p.me, d))
        self.layer_out(0)

    def steps(self):
        p = self.place
        if self.z_relay:
            self.got(0, 1, self.mine(1, 0))
            self.send(0, 3, self.mine(1, 0), p.layer(p.me, 2))
            self.layer_out(1)
            yield
        self.got(0, 2, self.mine(2, 0))
        self.layer_out(2)
        yield
        if not self.z_relay:
            self.got(0, 1, self.mine(1, 0))
            self.layer_out(1)
            yield
        self.got(0, 3, self.mine(3, 0))
        self.layer_out(3)
        yield
        if self.p_relay:
            for d in (0, 1, 2, 3):
                self.from_plane(d, (1,))
            yield
            for d in (0, 1, 2, 3):
                self.from_plane(d, (2, 3))
                yield
        else:
            for d in (0, 2, 1, 3):
                self.from_plane(d)
                yield

    def finish(self):
        for d in range(4):
            for k in range(4):
                self.got(2, d * 4 + k, self.theirs(d, k))

    def sent(self):
        for copy in self.sends:
            copy.wait_send()


def gather_sems():
    return [pltpu.SemaphoreType.DMA((size,)) for size in (4, 4, 16, 16, 16, 16)]


class Exchange:
    def __init__(self, n, me, src, dst, piece, send, recv):
        self.me, self.src, self.dst, self.half = me, src, dst, n // 2
        self.rows, self.first = pl.ds(piece * 16, 16), piece * n
        self.send, self.recv = send, recv
        self.home = me // self.half * self.half
        self.away = self.half - self.home

    def copy(self, base, k, slot):
        out = base + lax.rem(self.me + k, self.half)
        return pltpu.make_async_remote_copy(
            src_ref=self.src.at[out, self.rows],
            dst_ref=self.dst.at[self.me, self.rows],
            send_sem=self.send.at[slot],
            recv_sem=self.recv.at[slot],
            device_id={"dap": out},
            device_id_type=MESH,
        )

    def arrival(self, base, k, slot):
        come = base + lax.rem(self.me + self.half - k, self.half)
        return pltpu.make_async_remote_copy(
            src_ref=self.src.at[come, self.rows],
            dst_ref=self.dst.at[come, self.rows],
            send_sem=self.send.at[slot],
            recv_sem=self.recv.at[slot],
            device_id={"dap": come},
            device_id_type=MESH,
        )

    def each(self, act):
        def away(k, carry):
            act(self.away, k, self.first + k)
            return carry

        def home(k, carry):
            act(self.home, k, self.first + self.half + k)
            return carry

        return functools.partial(lax.fori_loop, 0, self.half, away, 0), functools.partial(
            lax.fori_loop, 1, self.half, home, 0
        )

    def start_away(self):
        self.each(lambda *at: self.copy(*at).start())[0]()

    def start_home(self):
        self.each(lambda *at: self.copy(*at).start())[1]()
        self.dst[self.me, self.rows] = self.src[self.me, self.rows]

    def start(self):
        self.start_away()
        self.start_home()

    def finish(self):
        away, home = self.each(lambda *at: self.arrival(*at).wait_recv())
        home()
        away()

    def sent(self):
        away, home = self.each(lambda *at: self.copy(*at).wait_send())
        home()
        away()


def iotas(rows, columns):
    shape = (rows, columns)
    return lax.broadcasted_iota(jnp.int32, shape, 0), lax.broadcasted_iota(jnp.int32, shape, 1)


def ones_where(condition):
    return condition.astype(full).astype(narrow)


def softmax(scores):
    powers = jnp.exp2(scores - jnp.max(scores, axis=-1, keepdims=True))
    return (powers * (1.0 / jnp.sum(powers, axis=-1, keepdims=True))).astype(narrow)


def attend(joint, gated, keeps, width, between):
    groups = len(keeps)
    length = joint.shape[0] // groups
    side = width // 2
    some = HEADS // 2
    lanes = lax.broadcasted_iota(jnp.int32, (length, side), 1) // HEAD
    picks = [ones_where(lanes == h) for h in range(some)]
    totals = []
    for g in range(groups):
        part = slice(g * length, (g + 1) * length)
        sides = []
        for first in (0, side):
            queries, keys_all = joint[part, first : first + side], joint[part, width + first : width + first + side]
            asked = jnp.concatenate([queries * pick for pick in picks], axis=0)
            scores = dot_nt(asked, keys_all) * SCALE
            weights = softmax(jnp.where(keeps[g], scores, MASKED))
            mixed = dot(weights, gated[part, first : first + side])
            total = mixed[:length]
            for h in range(1, some):
                total = jnp.where(lanes == h, mixed[h * length : (h + 1) * length], total)
            sides.append(total)
            between()
        totals.append(jnp.concatenate(sides, axis=1))
    total = jnp.concatenate(totals, axis=0)
    return (total * jax.nn.sigmoid(gated[:, width:].astype(full))).astype(narrow)


N_IN = 17
PARTS = 2


def kernel(n, *refs):
    inputs, (new_alignment, new_pair), scratch = refs[:N_IN], refs[N_IN : N_IN + 2], refs[N_IN + 2 :]
    held, scratch = scratch[:N_IN], scratch[N_IN:]
    (
        bias_a, bias_b, wide_bias, joints, asked_all, gate_all, mixed_all, residual, spread_a,
        spread_b, spread_both, back_a, back_b, sent, columns, new_sent, back, left, right_a, right_b,
        wide_right, products, outer_a, wide_output, turned_output, in_sems,
        to_send, to_recv, back_send, back_recv, *sems,
    ) = scratch
    (
        alignment, pair_rep, align_mask, residue_mask, row_gain, pair_gain, row_bias, row_scoring,
        row_values, row_output, column_gain, column_scoring, column_values, column_output,
        outer_gain, outer_inputs, outer_output,
    ) = held
    me = lax.axis_index("dap")
    place = Place(me)
    seqs, total_res, width = alignment.shape
    rows = pair_rep.shape[0]
    channels = pair_rep.shape[2]
    total_seqs = seqs * n
    half = rows // 2
    block = seqs * half

    order = (1, 5, 6, 2, 0, 4, 7, 8, 3, 9, 10, 11, 12, 13, 14, 15, 16)
    loads = [pltpu.make_async_copy(inputs[k], held[k], in_sems.at[k]) for k in range(N_IN)]
    for k in order:
        loads[k].start()
    greet(place)

    for k in (1, 5, 6, 2):
        loads[k].wait()
    biases = []
    for i in range(rows):
        normed = norm(pair_rep[i].astype(full), pair_gain[...])
        biases.append(dot_nt(row_bias[...], normed))
    biases = jnp.concatenate(biases, axis=0).astype(narrow)
    r, c = iotas(rows * HEADS, rows * HEADS)
    piece_of, rest = r // (half * HEADS), r % (half * HEADS)
    biases = dot(ones_where(c == (piece_of * half + rest % half) * HEADS + rest // half), biases).astype(narrow)
    bias_a[me] = biases[: half * HEADS]
    bias_b[me, : half * HEADS] = biases[half * HEADS :]
    mask_rows = jnp.concatenate([align_mask[...].astype(full), jnp.zeros((16 - seqs, total_res), full)], axis=0)
    bias_b[me, half * HEADS :] = mask_rows.astype(narrow)
    met(place)
    gather_a = Gather(place, bias_a, sems[:6], False, False)
    gather_b = Gather(place, bias_b, sems[6:12], False, False)
    gather_a.start()
    steps_a, steps_b = gather_a.steps(), gather_b.steps()

    for k in (0, 4, 7, 8):
        loads[k].wait()
    r, c = iotas(total_res, total_res)
    lane_head = c[: total_res // 2, : width // 2] // HEAD
    row_half = r[: total_res // 2, : width // 2] % rows // half
    kept = [lane_head == 2 * hp + row_half for hp in range(2)]
    pair_masks = [ones_where(k) for k in kept]
    doubles = [ones_where(c == r // rows * rows + piece * half + r % half) for piece in range(2)]

    def project(s):
        normed = norm(alignment[s].astype(full), row_gain[...])
        joint = dot(normed, row_scoring[...]).astype(narrow)
        gated = dot(normed, row_values[...]).astype(narrow)
        joints[s, :, :width] = joint[:, width:]
        joints[s, :, width:] = gated[:, :width]
        for piece in range(2):
            asked_all[piece, s] = dot(doubles[piece], joint[:, :width]).astype(narrow)
            gate_all[piece, s] = jax.nn.sigmoid(dot(doubles[piece], gated[:, width:]))

    for s in range(seqs):
        project(s)
        if s == 1:
            for _ in range(3):
                next(steps_a, None)
            gather_b.start()
    for k in (3, 9, 10, 11, 12, 13, 14, 15, 16):
        loads[k].wait()

    r, c = iotas(n * block, seqs * total_res)
    same = (r % block // half == c // total_res) & (r // block == c % total_res // rows) & (r % half == c % half)
    spread_a[...] = ones_where(same & (c % rows < half))
    spread_b[...] = ones_where(same & (c % rows >= half))
    spreads = (spread_a, spread_b)
    next(steps_a, None)
    next(steps_a, None)
    for _ in range(3):
        next(steps_b, None)
    r, c = iotas(n * block // 2, seqs * total_res // 2)
    same = (r % block // half == c // (total_res // 2)) & (r // block == c % (total_res // 2) // rows)
    spread_both[...] = ones_where(same & (r % half == c % half))
    flat_alignment = alignment[...].reshape(seqs * total_res, width)
    for piece in range(2):
        residual[piece] = dot(spreads[piece][...], flat_alignment)
    next(steps_a, None)
    r, c = iotas(seqs * total_res, n * block)
    same = (c % block // half == r // total_res) & (c // block == r % total_res // rows) & (c % half == r % half)
    back_a[...] = ones_where(same & (r % rows < half))
    back_b[...] = ones_where(same & (r % rows >= half))
    for _ in steps_a:
        pass

    wide_output[...] = outer_output[...].astype(full).reshape(wide_output.shape)
    for g in range(C_OPM // 8):
        for parity in range(2):
            block_of = [wide_output[:, 2 * (g * 4 + t) + parity, :] for t in range(4)]
            turned_output[parity * channels : (parity + 1) * channels, g * 128 : (g + 1) * 128] = (
                jnp.concatenate(block_of, axis=0).T.astype(narrow)
            )
    gather_a.finish()

    residue_float = residue_mask[...].astype(full)
    bias_blocks = (bias_a, bias_b)
    keeps = [align_mask[s : s + 1, :].astype(full) * residue_float > 0 for s in range(seqs)]

    count = n // 2
    side = width // 2

    def row_part(piece, base, between):
        wide = bias_blocks[piece][pl.ds(base, count), : half * HEADS, :].astype(full) * LOG2E
        wide_bias[...] = wide
        doubled = pl.ds(pl.multiple_of(base * rows, count * rows), count * rows)
        for s in range(seqs):
            keys_all, values_all = joints[s, :, :width], joints[s, :, width:]
            queries = asked_all[piece, s, doubled, :]
            sides = []
            for hp in range(HEADS // 2):
                lanes_here = slice(hp // 2 * side, (hp // 2 + 1) * side)
                asked = queries[:, lanes_here] * pair_masks[hp % 2]
                bias = wide_bias[:, hp * rows : (hp + 1) * rows, :].reshape(count * rows, total_res)
                scores = dot_nt(asked, keys_all[:, lanes_here]) * SCALE + bias
                weights = softmax(jnp.where(keeps[s], scores, MASKED))
                mixed = dot(weights, values_all[:, lanes_here])
                if hp % 2:
                    sides[-1] = jnp.where(kept[1], mixed, sides[-1])
                else:
                    sides.append(jnp.where(kept[0], mixed, 0.0))
            total = jnp.concatenate(sides, axis=1)
            here = slice(s * count * rows, (s + 1) * count * rows)
            mixed_all[here, :] = (total * gate_all[piece, s, doubled, :]).astype(narrow)
            between()
        mixed = dot(spread_both[...], mixed_all[...]).astype(narrow)
        start = pl.multiple_of(base * block, count * block)
        updated = residual[piece, pl.ds(start, count * block), :] + dot(mixed, row_output[...])
        sent[pl.ds(base, count), piece * block : (piece + 1) * block, :] = (
            updated.astype(narrow).reshape(count, block, width)
        )

    def row_piece(piece, between):
        exchange = Exchange(n, me, sent, columns, piece, to_send, to_recv)
        row_part(piece, exchange.away, lambda: None)
        exchange.start_away()
        row_part(piece, exchange.home, between)
        exchange.start_home()
        return exchange

    def relay_b():
        next(steps_b, None)

    to_a = row_piece(0, relay_b)
    for _ in steps_b:
        pass
    gather_b.finish()
    to_b = row_piece(1, lambda: None)

    every_mask = bias_b[:, half * HEADS :, :].reshape(n * 16, total_res)
    r, c = iotas(total_seqs, n * 16)
    mask = dot(ones_where(c == r // seqs * 16 + r % seqs), every_mask).astype(narrow)
    r, c = iotas(rows, total_res)
    own = ones_where(c == me * rows + r)
    keep_columns = dot_nt(own, mask)
    row_factor = jnp.sum(own.astype(full) * residue_float, axis=-1, keepdims=True)
    pair_count = dot(keep_columns.astype(narrow), mask)
    scale = row_factor * residue_float / (0.001 + pair_count)

    length = half * total_seqs
    r, c = iotas(length, length)
    into = ones_where(c == r % total_seqs * half + r // total_seqs)
    out_of = ones_where(r == c % total_seqs * half + c // total_seqs)
    r, c = iotas(C_OPM * half, C_OPM * half)
    by_channel = ones_where(c == r % half * C_OPM + r // half)
    rights = (right_a, right_b)

    def column_piece(piece, between):
        rows_here = pl.ds(piece * block, block)
        stream = dot(into, columns[:, rows_here].reshape(length, width))
        normed = norm(stream, column_gain[...])
        joint = dot(normed, column_scoring[...]).astype(narrow)
        gated = dot(normed, column_values[...]).astype(narrow)
        mine = range(piece * half, (piece + 1) * half)
        mixed = attend(joint, gated, [keep_columns[i : i + 1, :] > 0 for i in mine], width, between)
        second = (stream + dot(mixed, column_output[...])).astype(narrow)
        outer_normed = norm(second.astype(full), outer_gain[...])
        right = []
        for t, i in enumerate(mine):
            part = slice(t * total_seqs, (t + 1) * total_seqs)
            sides = dot_nt(outer_inputs[...], outer_normed[part]) * keep_columns[i : i + 1, :]
            left[i] = sides[:C_OPM].astype(narrow)
            right.append(sides[C_OPM:].astype(narrow))
        rights[piece][me] = dot(by_channel, jnp.concatenate(right, axis=0)).astype(narrow)
        gather = Gather(place, rights[piece], sems[12 + 6 * piece : 18 + 6 * piece], False, False)
        gather.start()
        new_sent[:, rows_here] = dot(out_of, second).astype(narrow).reshape(n, block, width)
        steps = gather.steps()
        for _ in range(3):
            next(steps, None)
        exchange = Exchange(n, me, new_sent, back, piece, back_send, back_recv)
        exchange.start()
        return gather, steps, exchange

    to_a.finish()
    right_a_gather, steps_a, home_a = column_piece(0, lambda: None)
    next(steps_a, None)
    to_b.finish()
    right_b_gather, steps_b, home_b = column_piece(1, lambda: None)
    for _ in steps_a:
        pass

    sides = left[...].reshape(rows * C_OPM, total_seqs)

    def outer(piece):
        wide_right[...] = rights[piece][...].astype(full)
        for e in range(C_OPM // 2):
            some = wide_right[:, e * rows : (e + 1) * rows, :].reshape(total_res, total_seqs)
            product = dot_nt(sides, some.astype(narrow)).astype(narrow)
            products[:, e * C_OPM : (e + 1) * C_OPM, :] = product.reshape(rows, C_OPM, total_res)
        for i in range(rows):
            yield i, dot(turned_output[...], products[i])

    low = lax.broadcasted_iota(jnp.int32, (1, total_res), 1) % rows < half
    next(steps_b, None)
    right_a_gather.finish()
    for i, first in outer(0):
        moved = pltpu.roll(first[channels:], total_res - half, 1)
        outer_a[i] = jnp.where(low, first[:channels] + moved, 0.0)
        if i in (0, 2, 4, 6):
            next(steps_b, None)
    for _ in steps_b:
        pass
    home_a.finish()
    flat_a = dot(back_a[...], back[:, :block].reshape(n * block, width))
    new_alignment[...] = flat_a.astype(narrow).reshape(new_alignment.shape)
    right_b_gather.finish()
    for i, second in outer(1):
        moved = pltpu.roll(second[:channels], half, 1)
        flat = (outer_a[i] + jnp.where(low, 0.0, second[channels:] + moved)) * scale[i : i + 1, :]
        new_pair[i] = (pair_rep[i].astype(full) + flat.T).astype(narrow)
    home_b.finish()
    flat_b = dot(back_b[...], back[:, block:].reshape(n * block, width))
    new_alignment[...] = (new_alignment[...].astype(full) + flat_b.reshape(new_alignment.shape)).astype(narrow)
    for exchange in (to_a, to_b, home_a, home_b):
        exchange.sent()
    for gather in (gather_a, gather_b, right_a_gather, right_b_gather):
        gather.sent()


def publish(first, second, first_out, second_out, first_held, second_held, arrived, done):
    ins, outs = [], []
    for k, (source, held, target) in enumerate(
        ((first, first_held, first_out), (second, second_held, second_out))
    ):
        size = source.shape[0] // PARTS
        for part in range(PARTS):
            here = pl.ds(part * size, size)
            ins.append(pltpu.make_async_copy(source.at[here], held.at[here], arrived.at[k, part]))
            outs.append(pltpu.make_async_copy(held.at[here], target.at[here], done.at[k, part]))
    for copy in ins:
        copy.start()
    for copy, onward in zip(ins, outs):
        copy.wait()
        onward.start()
    for copy in outs:
        copy.wait()


def body(n, alignment, pair_rep, align_mask, residue_mask, *rest):
    (
        row_gain, pair_gain, row_bias, row_scoring, row_values, row_output, column_gain,
        column_scoring, column_values, column_output, outer_gain, outer_inputs, outer_output,
    ) = rest
    seqs, total_res, width = alignment.shape
    rows, _, channels = pair_rep.shape
    total_seqs = seqs * n
    half = rows // 2
    arguments = (
        alignment, pair_rep, align_mask, residue_mask[None], row_gain[None], pair_gain[None],
        row_bias.T, row_scoring, row_values, row_output, column_gain[None], column_scoring,
        column_values, column_output, outer_gain[None], outer_inputs.T, outer_output,
    )
    dma = pltpu.SemaphoreType.DMA
    blocks = (n, seqs * rows, width)
    sent = n * seqs * half
    right_shape = (n, C_OPM * half, total_seqs)
    results = pl.pallas_call(
        functools.partial(kernel, n),
        out_shape=(
            jax.ShapeDtypeStruct(alignment.shape, narrow),
            jax.ShapeDtypeStruct(pair_rep.shape, narrow),
        ),
        in_specs=[pl.BlockSpec(memory_space=pltpu.HBM)] * N_IN,
        out_specs=(VMEM, VMEM),
        scratch_shapes=[pltpu.VMEM(array.shape, array.dtype) for array in arguments]
        + [
            pltpu.VMEM((n, HEADS * half, total_res), narrow),
            pltpu.VMEM((n, HEADS * half + 16, total_res), narrow),
            pltpu.VMEM((n // 2, HEADS * half, total_res), full),
            pltpu.VMEM((seqs, total_res, 2 * width), narrow),
            pltpu.VMEM((2, seqs, total_res, width), narrow),
            pltpu.VMEM((2, seqs, total_res, width), full),
            pltpu.VMEM((seqs * total_res // 2, width), narrow),
            pltpu.VMEM((2, sent, width), full),
            pltpu.VMEM((sent, seqs * total_res), narrow),
            pltpu.VMEM((sent, seqs * total_res), narrow),
            pltpu.VMEM((sent // 2, seqs * total_res // 2), narrow),
            pltpu.VMEM((seqs * total_res, sent), narrow),
            pltpu.VMEM((seqs * total_res, sent), narrow),
            pltpu.VMEM(blocks, narrow),
            pltpu.VMEM(blocks, narrow),
            pltpu.VMEM(blocks, narrow),
            pltpu.VMEM(blocks, narrow),
            pltpu.VMEM((rows, C_OPM, total_seqs), narrow),
            pltpu.VMEM(right_shape, narrow),
            pltpu.VMEM(right_shape, narrow),
            pltpu.VMEM(right_shape, full),
            pltpu.VMEM((rows, C_OPM * C_OPM // 2, total_res), narrow),
            pltpu.VMEM((rows, channels, total_res), full),
            pltpu.VMEM((C_OPM, C_OPM, channels), full),
            pltpu.VMEM((2 * channels, C_OPM * C_OPM // 2), narrow),
            dma((N_IN,)),
        ]
        + [dma((2 * n,))] * 4
        + gather_sems() * 4,
        compiler_params=pltpu.CompilerParams(
            vmem_limit_bytes=LIMIT, collective_id=0, has_side_effects=True
        ),
        name="evoformer",
    )(*arguments)
    return pl.pallas_call(
        publish,
        out_shape=[jax.ShapeDtypeStruct(array.shape, narrow) for array in results],
        in_specs=[pl.BlockSpec(memory_space=pl.ANY)] * 2,
        out_specs=[pl.BlockSpec(memory_space=pl.ANY)] * 2,
        scratch_shapes=[pltpu.VMEM(array.shape, narrow) for array in results] + [dma((2, PARTS))] * 2,
        name="publish",
    )(*results)


def solution(mesh):
    split = P(("dp", "dap"), None, None)
    in_specs = (split, split, P(("dp", "dap"), None), P("dp")) + (P(),) * 13
    return jax.shard_map(
        functools.partial(body, mesh.shape["dap"]),
        mesh=mesh,
        in_specs=in_specs,
        out_specs=(split, split),
        check_vma=False,
    )
```
